128 devices in a mesh: row: 8 (over z_lo, x), col: 16 (over y, z_hi, core).
Axes of the slice: x: 4, y: 4, z: 4 (z_hi: 2, z_lo: 2; z = z_hi * 2 + z_lo), core: 2. Of those that a mesh axis runs over, the one named last changes fastest.
Arguments:
- eigenvectors: bfloat16 [28672, 28672], P('col', 'row'), may hold values from -0.75 to 0.75
- reflectors_first: bfloat16 [28672, 256], P(('row', 'col')), may hold values from -600 to 600, as said below
- reflectors_second: bfloat16 [28672, 256], P(('row', 'col')), may hold values from -600 to 600, as said below
- forget_gradient: bfloat16 [256, 28672], P(None, ('row', 'col')), may hold values from -0.03125 to 0.03125
Outputs:
- eigenvectors_new: bfloat16 [28672, 28672], P(('col', 'row'))
- rotated_gradient: bfloat16 [28672, 256], P(('col', 'row'))
The draws below stay inside these ranges and needn't reach their ends.
Inputs may be any that keep to these rules, and one draw needn't show every extreme that they name: `reflectors_first`: the columns are the vectors of 256 Householder reflectors. `reflectors_second`: the columns are the vectors of 256 Householder reflectors.
All inputs are finite; a program needn't handle non-finite values.
Results may differ from the reference program's by a relative error of at most 0.0051.
Values may be sent and summed in bfloat16 or wider, within the bound.
A program may use at most 128 MiB of HBM per device.

```python
import math
import jax
import jax.numpy as jnp
from jax import lax

N = 28672
B = 256
ROWS = 256
N_ROW = 8
N_COL = 16


def reflector_draw(key, member):
    column_key = jax.random.fold_in(key, 101 + member)
    independent_key = jax.random.fold_in(key, 201 + member)
    common_key = jax.random.fold_in(key, 301)
    row_key = jax.random.fold_in(key, 401)
    column_scale = jnp.exp(jax.random.uniform(column_key, (1, B), jnp.float32, 0.0, math.log(10.0)))
    rising = 1.0 + 2.0 * jnp.arange(N, dtype=jnp.float32)[:, None] / N
    row_scale = rising * jnp.exp(jax.random.uniform(row_key, (N, 1), jnp.float32, 0.0, math.log(3.4)))
    independent = jnp.clip(jax.random.normal(independent_key, (N, B), jnp.float32), -4.0, 4.0)
    common = jnp.clip(jax.random.normal(common_key, (N, 1), jnp.float32), -4.0, 4.0)
    blended = 0.9 * independent + 0.45 * common
    return (blended * row_scale * column_scale).astype(jnp.bfloat16)


def draw_reflectors_first(key, part):
    return reflector_draw(key, 0)


def draw_reflectors_second(key, part):
    return reflector_draw(key, 1)


def shard_levels(own_key, dims, split, low, largest):
    loudness = 1.0
    for position, parts in split:
        draws = jax.random.uniform(jax.random.fold_in(jax.random.fold_in(own_key, 6), position), (parts,), jnp.float32, low / len(split), largest / len(split))
        loudness = loudness * jnp.repeat(jnp.exp(draws), dims[position] // parts).reshape((-1,) + (1,) * (len(dims) - 1 - position))
    return loudness


def centred(own_key, dims, deviation, reach, cuts=(), kind=jnp.bfloat16):
    drawn = deviation * jax.random.normal(own_key, dims, jnp.float32)
    if cuts:
        drawn = drawn * shard_levels(own_key, dims, cuts, -0.22, 0.18)
    return jnp.clip(drawn, -reach, reach).astype(kind)


def setup_inputs(seed: int = 0) -> dict:
    splits = jax.random.split(jax.random.key(seed), 5)
    return {
        "eigenvectors": centred(splits[0], (N, N), 0.125, 0.75, ((0, 16), (1, 8))),
        "reflectors_first": draw_reflectors_first(jax.random.fold_in(splits[4], 71), 0),
        "reflectors_second": draw_reflectors_second(jax.random.fold_in(splits[4], 71), 0),
        "forget_gradient": centred(splits[3], (ROWS, N), N ** -0.5, 0.03125, ((1, 128),)),
    }


def inner_products(left_side, right_side):
    return lax.dot_general(left_side, right_side, (((0,), (0,)), ((), ())), preferred_element_type=jnp.float32)


def upper_factor(gram_block):
    return jnp.triu(gram_block) - 0.5 * jnp.diag(jnp.diag(gram_block))


def upper_inverse(gram_block):
    factor = upper_factor(gram_block)
    order = factor.shape[0]
    identity = jnp.eye(order, dtype=factor.dtype)

    def backward_row(counter, inverse_rows):
        index = (order - 1 - counter).astype(jnp.int32)
        factor_row = lax.dynamic_slice_in_dim(factor, index, 1, 0)
        unit_row = lax.dynamic_slice_in_dim(identity, index, 1, 0)
        pivot_entry = lax.dynamic_slice(factor, (index, index), (1, 1))
        filled = jnp.dot(factor_row, inverse_rows, precision=lax.Precision.HIGHEST, preferred_element_type=factor.dtype)
        fresh_row = (unit_row - filled) / pivot_entry
        return lax.dynamic_update_slice_in_dim(inverse_rows, fresh_row, index, 0)

    return lax.fori_loop(0, order, backward_row, jnp.zeros_like(factor))


def solve_coefficients(products, gram_first, gram_second, cross_gram, block_width):
    inverse_first = upper_inverse(gram_first)
    inverse_second = upper_inverse(gram_second)
    coef_first = jnp.dot(products[:, :block_width], inverse_first, precision=lax.Precision.HIGHEST, preferred_element_type=jnp.float32)
    shifted = products[:, block_width:] - jnp.dot(coef_first, cross_gram, precision=lax.Precision.HIGHEST, preferred_element_type=jnp.float32)
    coef_second = jnp.dot(shifted, inverse_second, precision=lax.Precision.HIGHEST, preferred_element_type=jnp.float32)
    return jnp.concatenate([coef_first, coef_second], axis=1).astype(jnp.bfloat16)


def reference(eigenvectors, reflectors_first, reflectors_second, forget_gradient):
    both_sets = jnp.concatenate([reflectors_first, reflectors_second], axis=1)
    gram_first = inner_products(reflectors_first, reflectors_first)
    gram_second = inner_products(reflectors_second, reflectors_second)
    cross_gram = inner_products(reflectors_first, reflectors_second)
    blocks = eigenvectors.reshape(N_ROW * N_COL, N // (N_ROW * N_COL), N)

    def renew_block(eig_rows):
        products = jnp.dot(eig_rows, both_sets, preferred_element_type=jnp.float32)
        coefficients = solve_coefficients(products, gram_first, gram_second, cross_gram, B)
        update = lax.dot_general(coefficients, both_sets, (((1,), (1,)), ((), ())), preferred_element_type=jnp.float32)
        renewed = (eig_rows.astype(jnp.float32) - update).astype(jnp.bfloat16)
        rotated = lax.dot_general(renewed, forget_gradient, (((1,), (1,)), ((), ())), preferred_element_type=jnp.float32)
        return renewed, rotated.astype(jnp.bfloat16)

    renewed, rotated = lax.map(renew_block, blocks)
    return renewed.reshape(N, N), rotated.reshape(N, ROWS)
```

```python
import jax
import jax.numpy as jnp
from jax import lax
from jax.experimental import pallas as pl
from jax.experimental.pallas import tpu as pltpu
from jax.sharding import PartitionSpec as P

HIGH = lax.Precision.HIGHEST


def inner_products(left_side, right_side):
    return lax.dot_general(
        left_side, right_side, (((0,), (0,)), ((), ())), preferred_element_type=jnp.float32
    )


def exact(left_side, right_side):
    return jnp.dot(left_side, right_side, precision=HIGH, preferred_element_type=jnp.float32)


def inverse_kernel(gram_ref, inverse_ref):
    order = gram_ref.shape[0]
    half = order // 2
    gram = gram_ref[...]
    rows = lax.broadcasted_iota(jnp.int32, (half, half), 0)
    cols = lax.broadcasted_iota(jnp.int32, (half, half), 1)
    parts = [gram[:half, :half], gram[half:, half:]]
    inverses = [jnp.where(rows == cols, 2.0 / part, 0.0) for part in parts]
    for level in range(half.bit_length() - 1):
        row_block, col_block = lax.shift_right_logical(rows, level), lax.shift_right_logical(cols, level)
        corner = (row_block + 1 == col_block) & ((row_block & 1) == 0)
        corners = [jnp.where(corner, part, 0.0) for part in parts]
        steps = [exact(c, i) for c, i in zip(corners, inverses)]
        inverses = [i - exact(i, s) for i, s in zip(inverses, steps)]
    cross = exact(inverses[0], exact(gram[:half, half:], inverses[1]))
    inverse_ref[:half, :half] = inverses[0]
    inverse_ref[half:, half:] = inverses[1]
    inverse_ref[:half, half:] = -cross
    inverse_ref[half:, :half] = jnp.zeros((half, half), jnp.float32)


def block_inverse(gram):
    return pl.pallas_call(
        inverse_kernel,
        out_shape=jax.ShapeDtypeStruct(gram.shape, jnp.float32),
        in_specs=[pl.BlockSpec(memory_space=pltpu.VMEM)],
        out_specs=pl.BlockSpec(memory_space=pltpu.VMEM),
        compiler_params=pltpu.CompilerParams(vmem_limit_bytes=32 * 1024 * 1024),
        name="block_inverse",
    )(gram)


def body(eigenvectors, reflectors_first, reflectors_second, forget_gradient):
    own_sets = jnp.concatenate([reflectors_first, reflectors_second], axis=1)
    both_sets = lax.all_gather(own_sets, "col", axis=0, tiled=True)
    gram = lax.psum(inner_products(both_sets, both_sets), "row")
    products = jnp.dot(eigenvectors, both_sets, preferred_element_type=jnp.float32)
    products = lax.psum(products, "row")
    coefficients = exact(products, block_inverse(gram)).astype(jnp.bfloat16)
    update = lax.dot_general(
        coefficients, both_sets, (((1,), (1,)), ((), ())), preferred_element_type=jnp.float32
    )
    renewed = (eigenvectors.astype(jnp.float32) - update).astype(jnp.bfloat16)
    eig_slab = lax.all_to_all(renewed, "row", split_axis=0, concat_axis=1, tiled=True)
    rotated = lax.dot_general(
        eig_slab,
        lax.all_gather(forget_gradient, ("row", "col"), axis=1, tiled=True),
        (((1,), (1,)), ((), ())),
        preferred_element_type=jnp.float32,
    )
    return (eig_slab, rotated.astype(jnp.bfloat16))


def solution(mesh):
    return jax.shard_map(
        body,
        mesh=mesh,
        in_specs=(
            P("col", "row"),
            P(("row", "col"), None),
            P(("row", "col"), None),
            P(None, ("row", "col")),
        ),
        out_specs=(P(("col", "row"), None), P(("col", "row"), None)),
        check_vma=False,
    )
```

```python
import jax
import jax.numpy as jnp
from jax import lax
from jax.experimental import pallas as pl
from jax.experimental.pallas import tpu as pltpu
from jax.sharding import PartitionSpec as P

MESH = pl.DeviceIdType.MESH
PARTS = 7
SLOTS = 144


def place():
    row, col = lax.axis_index("row"), lax.axis_index("col")
    return row // 4, row % 4, col // 4, (col // 2) % 2, col % 2


def device(zl, x, y, zh, k):
    return (zl * 4 + lax.rem(x + 4, 4), lax.rem(y + 4, 4) * 4 + zh * 2 + k)


class Transfers:
    def __init__(self, send_sem, recv_sem):
        self.send_sem, self.recv_sem = send_sem, recv_sem
        self.count = 0
        self.pending_send, self.pending_recv = {}, {}

    def start(self, source, target, to, arrival=None):
        slot = self.count
        self.count += 1
        copy = pltpu.make_async_remote_copy(
            source, target, self.send_sem.at[slot], self.recv_sem.at[slot],
            device_id=to, device_id_type=MESH,
        )
        copy.start()
        self.pending_send[slot] = copy
        self.pending_recv[slot] = copy
        return slot

    def received(self, slot):
        if slot in self.pending_recv:
            self.pending_recv.pop(slot).wait_recv()

    def sent(self, slot):
        if slot in self.pending_send:
            self.pending_send.pop(slot).wait_send()

    def finish(self):
        for slot in list(self.pending_recv):
            self.received(slot)
        for slot in list(self.pending_send):
            self.sent(slot)


def comm_kernel(e_ref, s_ref, g_ref, x_ref, sf_ref, gf_ref, send_sem, recv_sem, local_sem):
    zl, x, y, zh, k = place()
    me = zl * 4 + x
    sib = device(zl, x, y, zh, 1 - k)
    cross = device(1 - zl, x, y, 1 - zh, k)
    partners = [device(a, x + d, y, zh, k) for a, d in
                [(1 - zl, 0), (zl, 1), (zl, 3), (1 - zl, 1), (1 - zl, 3), (zl, 2), (1 - zl, 2)]]
    barrier = pltpu.get_barrier_semaphore()
    everyone = partners + [sib, cross] + [device(zl, x, y + d, zh, k) for d in (1, 2, 3)]
    for to in everyone:
        pl.semaphore_signal(barrier, inc=1, device_id=to, device_id_type=MESH)
    pl.semaphore_wait(barrier, len(everyone))

    t = Transfers(send_sem, recv_sem)
    rows, width = x_ref.shape[0], e_ref.shape[1]

    own_columns = pl.ds(pl.multiple_of(me * width, 128), width)
    mine = pltpu.make_async_copy(
        e_ref.at[pl.ds(pl.multiple_of(me * rows, 16), rows)], x_ref.at[:, own_columns], local_sem.at[0])
    mine_s = pltpu.make_async_copy(s_ref, sf_ref.at[zl, x, y, zh, k], local_sem.at[1])
    mine_g = pltpu.make_async_copy(g_ref, gf_ref.at[zl, x, y, zh, k], local_sem.at[2])

    piece = rows // PARTS
    batches = []

    def batch():
        q = len(batches)
        slots = []
        if q < PARTS:
            for to in partners:
                theirs = to[0]
                src = e_ref.at[pl.ds(pl.multiple_of(theirs * rows + q * piece, 16), piece)]
                dst = x_ref.at[pl.ds(q * piece, piece), own_columns]
                slots.append(t.start(src, dst, to))
        batches.append(slots)

    def push(ref, index, to):
        view = ref.at[index]
        return t.start(view, view, to)

    def share(ref, index):
        return push(ref, index, sib)

    full = slice(None)
    mine_s.start()
    mine_g.start()
    mine.start()
    own = (zl, x, y, zh, k)
    a1 = t.start(s_ref, sf_ref.at[own], device(1 - zl, x, y, zh, k))
    a2a = [t.start(s_ref, sf_ref.at[own], device(zl, x + d, y, zh, k)) for d in (1, 3, 2)]
    b1 = [t.start(g_ref, gf_ref.at[own], device(zl, x + d, y, zh, k)) for d in (1, 3, 2)]
    t.start(s_ref, sf_ref.at[own], sib)
    t.start(g_ref, gf_ref.at[own], sib)
    batch()
    mine_s.wait()
    mine_g.wait()
    t.received(a1)
    other = (1 - zl, x, y, zh, k)
    a2b = [push(sf_ref, other, device(zl, x + d, y, zh, k)) for d in (1, 3, 2)]
    for s in a2a:
        t.received(s)
    a3a = push(sf_ref, (zl, full, y, zh, k), cross)
    a4a = [[push(sf_ref, (zl, full, y, zh, k), device(zl, x, y + d, zh, k)) for d in (1, 3)]]
    for s in b1:
        t.received(s)
    b2 = push(gf_ref, (zl, full, y, zh, k), device(1 - zl, x, y, zh, k))
    for s in a2b:
        t.received(s)
    a3b = push(sf_ref, (1 - zl, full, y, zh, k), cross)
    a4a.append([push(sf_ref, (1 - zl, full, y, zh, k), device(zl, x, y + d, zh, k)) for d in (1, 3)])
    t.received(b2)
    b3 = {d: push(gf_ref, (full, full, y, zh, k), device(zl, x, y + d, zh, k)) for d in (1, 3, 2)}
    b4 = [push(gf_ref, (full, full, y, zh, k), cross)]
    for d in (1, 2, 3):
        share(sf_ref, (full, lax.rem(x + d, 4), y, zh, k))
        share(gf_ref, (full, lax.rem(x + d, 4), y, zh, k))
    share(sf_ref, other)
    share(gf_ref, other)
    batch()
    t.received(a3a)
    a4b = [[push(sf_ref, (1 - zl, full, y, 1 - zh, k), device(zl, x, y + d, zh, k)) for d in (1, 3)]]
    t.received(a3b)
    a4b.append([push(sf_ref, (zl, full, y, 1 - zh, k), device(zl, x, y + d, zh, k)) for d in (1, 3)])
    share(sf_ref, (full, full, y, 1 - zh, k))
    batch()
    up, down, far = lax.rem(y + 1, 4), lax.rem(y + 3, 4), lax.rem(y + 2, 4)
    source_of = {1: down, 3: up, 2: far}
    far_own, far_other = [], []
    for part, a in ((0, zl), (1, 1 - zl)):
        t.received(a4a[part][0])
        far_own.append(push(sf_ref, (a, full, down, zh, k), device(zl, x, y + 1, zh, k)))
    for d in (1, 3):
        t.received(b3[d])
        b4.append(push(gf_ref, (full, full, source_of[d], zh, k), cross))
        share(gf_ref, (full, full, source_of[d], zh, k))
    for part in (0, 1):
        t.received(a4a[part][1])
    share(sf_ref, (full, full, down, zh, k))
    share(sf_ref, (full, full, up, zh, k))
    batch()
    t.received(b3[2])
    b4.append(push(gf_ref, (full, full, far, zh, k), cross))
    share(gf_ref, (full, full, far, zh, k))
    batch()
    for part, a in ((0, 1 - zl), (1, zl)):
        t.received(a4b[part][1])
        far_other.append(push(sf_ref, (a, full, up, 1 - zh, k), device(zl, x, y + 3, zh, k)))
    t.received(b4[0])
    share(gf_ref, (full, full, y, 1 - zh, k))
    for part in (0, 1):
        t.received(a4b[part][0])
    share(sf_ref, (full, full, down, 1 - zh, k))
    share(sf_ref, (full, full, up, 1 - zh, k))
    batch()
    batch()
    for i, d in ((1, 1), (2, 3)):
        t.received(b4[i])
        share(gf_ref, (full, full, source_of[d], 1 - zh, k))
    for slot in far_own:
        t.received(slot)
    share(sf_ref, (full, full, far, zh, k))
    t.received(b4[3])
    share(gf_ref, (full, full, far, 1 - zh, k))
    for slot in far_other:
        t.received(slot)
    share(sf_ref, (full, full, far, 1 - zh, k))
    t.finish()
    mine.wait()


def exchange(eigenvectors, sets, gradient):
    blocks = (2, 4, 4, 2, 2)
    rows, width = eigenvectors.shape[0] // 8, eigenvectors.shape[1]
    return pl.pallas_call(
        comm_kernel,
        out_shape=(
            jax.ShapeDtypeStruct((rows, 8 * width), jnp.bfloat16),
            jax.ShapeDtypeStruct(blocks + sets.shape, jnp.bfloat16),
            jax.ShapeDtypeStruct(blocks + gradient.shape, jnp.bfloat16),
        ),
        in_specs=[pl.BlockSpec(memory_space=pl.ANY)] * 3,
        out_specs=(pl.BlockSpec(memory_space=pl.ANY),) * 3,
        scratch_shapes=[
            pltpu.SemaphoreType.DMA((SLOTS,)),
            pltpu.SemaphoreType.DMA((SLOTS,)),
            pltpu.SemaphoreType.DMA((3,)),
        ],
        compiler_params=pltpu.CompilerParams(
            collective_id=0, has_side_effects=True, vmem_limit_bytes=48 * 1024 * 1024
        ),
        name="exchange",
    )(eigenvectors, sets, gradient)


HIGH = lax.Precision.HIGHEST


def inner_products(left_side, right_side):
    return lax.dot_general(
        left_side, right_side, (((0,), (0,)), ((), ())), preferred_element_type=jnp.float32
    )


def exact(left_side, right_side):
    return jnp.dot(left_side, right_side, precision=HIGH, preferred_element_type=jnp.float32)


def inverse_kernel(gram_ref, inverse_ref):
    order = gram_ref.shape[0]
    half = order // 2
    gram = gram_ref[...]
    rows = lax.broadcasted_iota(jnp.int32, (half, half), 0)
    cols = lax.broadcasted_iota(jnp.int32, (half, half), 1)
    parts = [gram[:half, :half], gram[half:, half:]]
    inverses = [jnp.where(rows == cols, 2.0 / part, 0.0) for part in parts]
    for level in range(half.bit_length() - 1):
        row_block, col_block = lax.shift_right_logical(rows, level), lax.shift_right_logical(cols, level)
        corner = (row_block + 1 == col_block) & ((row_block & 1) == 0)
        corners = [jnp.where(corner, part, 0.0) for part in parts]
        steps = [exact(c, i) for c, i in zip(corners, inverses)]
        inverses = [i - exact(i, s) for i, s in zip(inverses, steps)]
    cross = exact(inverses[0], exact(gram[:half, half:], inverses[1]))
    inverse_ref[:half, :half] = inverses[0]
    inverse_ref[half:, half:] = inverses[1]
    inverse_ref[:half, half:] = -cross
    inverse_ref[half:, :half] = jnp.zeros((half, half), jnp.float32)


def block_inverse(gram):
    return pl.pallas_call(
        inverse_kernel,
        out_shape=jax.ShapeDtypeStruct(gram.shape, jnp.float32),
        in_specs=[pl.BlockSpec(memory_space=pltpu.VMEM)],
        out_specs=pl.BlockSpec(memory_space=pltpu.VMEM),
        compiler_params=pltpu.CompilerParams(vmem_limit_bytes=32 * 1024 * 1024),
        name="block_inverse",
    )(gram)


def body(eigenvectors, reflectors_first, reflectors_second, forget_gradient):
    own_sets = jnp.concatenate([reflectors_first, reflectors_second], axis=1)
    slab, all_sets, all_gradient = exchange(eigenvectors, own_sets, forget_gradient.T)
    all_sets = all_sets.reshape(-1, own_sets.shape[1])
    all_gradient = all_gradient.reshape(-1, forget_gradient.shape[0])
    gram = inner_products(all_sets, all_sets)
    products = jnp.dot(slab, all_sets, preferred_element_type=jnp.float32)
    coefficients = exact(products, block_inverse(gram)).astype(jnp.bfloat16)
    update = lax.dot_general(
        coefficients, all_sets, (((1,), (1,)), ((), ())), preferred_element_type=jnp.float32
    )
    renewed = (slab.astype(jnp.float32) - update).astype(jnp.bfloat16)
    rotated = jnp.dot(renewed, all_gradient, preferred_element_type=jnp.float32)
    return (renewed, rotated.astype(jnp.bfloat16))


def solution(mesh):
    return jax.shard_map(
        body,
        mesh=mesh,
        in_specs=(
            P("col", "row"),
            P(("row", "col"), None),
            P(("row", "col"), None),
            P(None, ("row", "col")),
        ),
        out_specs=(P(("col", "row"), None), P(("col", "row"), None)),
        check_vma=False,
    )
```

```python
import jax
import jax.numpy as jnp
from jax import lax
from jax.experimental import pallas as pl
from jax.experimental.pallas import tpu as pltpu
from jax.sharding import PartitionSpec as P

MESH = pl.DeviceIdType.MESH
HIGH = lax.Precision.HIGHEST
BATCHES = 7
SLOTS = 160
SPLIT = 384
UPPER = 128


def exact(left_side, right_side):
    return jnp.dot(left_side, right_side, precision=HIGH, preferred_element_type=jnp.float32)


def inner_products(left_side, right_side):
    return lax.dot_general(
        left_side, right_side, (((0,), (0,)), ((), ())), preferred_element_type=jnp.float32
    )


def invert_upper(gram, inverse_ref):
    half = gram.shape[0] // 2
    rows = lax.broadcasted_iota(jnp.int32, (half, half), 0)
    cols = lax.broadcasted_iota(jnp.int32, (half, half), 1)
    parts = [gram[:half, :half], gram[half:, half:]]
    inverses = [jnp.where(rows == cols, 2.0 / part, 0.0) for part in parts]
    for level in range(half.bit_length() - 1):
        row_block, col_block = lax.shift_right_logical(rows, level), lax.shift_right_logical(cols, level)
        corner = (row_block + 1 == col_block) & ((row_block & 1) == 0)
        corners = [jnp.where(corner, part, 0.0) for part in parts]
        steps = [exact(c, i) for c, i in zip(corners, inverses)]
        inverses = [i - exact(i, s) for i, s in zip(inverses, steps)]
    cross = exact(inverses[0], exact(gram[:half, half:], inverses[1]))
    inverse_ref[:half, :half] = inverses[0]
    inverse_ref[half:, half:] = inverses[1]
    inverse_ref[:half, half:] = -cross
    inverse_ref[half:, :half] = jnp.zeros((half, half), jnp.float32)


def place():
    row, col = lax.axis_index("row"), lax.axis_index("col")
    return row // 4, row % 4, col // 4, (col // 2) % 2, col % 2


def device(zl, x, y, zh, k):
    return (zl * 4 + lax.rem(x + 4, 4), lax.rem(y + 4, 4) * 4 + zh * 2 + k)


class Transfers:
    def __init__(self, send_sem, recv_sem):
        self.send_sem, self.recv_sem = send_sem, recv_sem
        self.count = 0
        self.pending_send, self.pending_recv = {}, {}

    def start(self, source, target, to):
        slot = self.count
        self.count += 1
        copy = pltpu.make_async_remote_copy(
            source, target, self.send_sem.at[slot], self.recv_sem.at[slot],
            device_id=to, device_id_type=MESH,
        )
        copy.start()
        self.pending_send[slot] = copy
        self.pending_recv[slot] = copy
        return slot

    def received(self, *slots):
        for slot in slots:
            if slot in self.pending_recv:
                self.pending_recv.pop(slot).wait_recv()

    def finish(self):
        self.received(*list(self.pending_recv))
        for copy in self.pending_send.values():
            copy.wait_send()


def exchange_kernel(
    e_ref, s_ref, g_ref, x_ref, sf_ref, gf_ref, coef_ref, rot_ref,
    send_sem, recv_sem, local_sem, part, from_y, y_sum, from_z, sums, inverse, total,
):
    zl, x, y, zh, k = place()
    me = zl * 4 + x
    sib = device(zl, x, y, zh, 1 - k)
    cross = device(1 - zl, x, y, 1 - zh, k)
    flip = device(zl, x, y, 1 - zh, k)
    other_z = device(1 - zl, x, y, zh, k)
    near_x = [device(zl, x + d, y, zh, k) for d in (1, 3, 2)]
    near_y = {d: device(zl, x, y + d, zh, k) for d in (1, 3, 2)}
    partners = [device(a, x + d, y, zh, k) for a, d in
                [(1 - zl, 0), (zl, 1), (zl, 3), (1 - zl, 1), (1 - zl, 3), (zl, 2), (1 - zl, 2)]]
    barrier = pltpu.get_barrier_semaphore()
    everyone = partners + [sib, cross, flip] + list(near_y.values())
    for to in everyone:
        pl.semaphore_signal(barrier, inc=1, device_id=to, device_id_type=MESH)
    pl.semaphore_wait(barrier, len(everyone))

    t = Transfers(send_sem, recv_sem)
    rows, width = x_ref.shape[0], e_ref.shape[1]
    own_columns = pl.ds(pl.multiple_of(me * width, 128), width)
    piece = rows // BATCHES
    batches = []
    full = slice(None)

    def batch():
        q = len(batches)
        slots = []
        for to in partners:
            source = e_ref.at[pl.ds(pl.multiple_of(to[0] * rows + q * piece, 16), piece)]
            slots.append(t.start(source, x_ref.at[pl.ds(q * piece, piece), own_columns], to))
        batches.append(slots)

    def push(ref, index, to):
        view = ref.at[index]
        return t.start(view, view, to)

    def share(ref, index):
        return push(ref, index, sib)

    mine = pltpu.make_async_copy(
        e_ref.at[pl.ds(pl.multiple_of(me * rows, 16), rows)], x_ref.at[:, own_columns], local_sem.at[0])
    mine_s = pltpu.make_async_copy(s_ref, sf_ref.at[zl, x, y, zh, k], local_sem.at[1])
    mine_g = pltpu.make_async_copy(g_ref, gf_ref.at[zl, x, y, zh, k], local_sem.at[2])

    def group_sums():
        part[...] = jnp.zeros_like(part)

        def step(s_block, g_block):
            s_value = s_block[...].reshape(-1, SPLIT)
            g_value = g_block[...].reshape(-1, g_block.shape[-1])
            sets = jnp.concatenate([s_value, g_value[:, :UPPER]], axis=1)
            part[:, :SPLIT] += inner_products(sets, s_value)
            part[:, SPLIT:] += inner_products(sets, g_value)

        def spec(ref):
            return pl.BlockSpec(
                (None, None, None, None, 2) + ref.shape[5:], lambda i: (i // 4, i % 4, y, zh, 0, 0, 0)
            )

        pltpu.emit_pipeline(step, grid=(8,), in_specs=[spec(sf_ref), spec(gf_ref)])(sf_ref, gf_ref)

    def add_products(y_block, low, high):
        def step(x_block, s_block, g_block):
            x_value = x_block[...]
            s_value = s_block[...].reshape(-1, SPLIT)
            g_value = g_block[...].reshape(-1, g_block.shape[-1])
            total[low:high, :SPLIT] += jnp.dot(x_value, s_value, preferred_element_type=jnp.float32)
            total[low:high, SPLIT:] += jnp.dot(x_value, g_value, preferred_element_type=jnp.float32)

        def spec(ref):
            return pl.BlockSpec(
                (None, None, None, 2, 2) + ref.shape[5:], lambda i: (i // 4, i % 4, y_block, 0, 0, 0, 0)
            )

        x_rows = x_ref.at[pl.ds(low, high - low)]
        x_spec = pl.BlockSpec((high - low, width // 4), lambda i: (0, i * 4 + y_block))
        pltpu.emit_pipeline(step, grid=(8,), in_specs=[x_spec, spec(sf_ref), spec(gf_ref)])(
            x_rows, sf_ref, gf_ref)

    mine_s.start()
    mine_g.start()
    own, other = (zl, x, y, zh, k), (1 - zl, x, y, zh, k)
    a1 = t.start(s_ref, sf_ref.at[own], other_z)
    a2a = [t.start(s_ref, sf_ref.at[own], to) for to in near_x]
    b1 = [t.start(g_ref, gf_ref.at[own], to) for to in near_x]
    home = [t.start(s_ref, sf_ref.at[own], sib), t.start(g_ref, gf_ref.at[own], sib)]
    batch()
    mine.start()
    total[...] = jnp.zeros_like(total)
    mine_s.wait()
    mine_g.wait()
    t.received(a1)
    a2b = [push(sf_ref, other, to) for to in near_x]
    t.received(*a2a)
    a3 = [push(sf_ref, (zl, full, y, zh, k), cross)]
    a4a = [[push(sf_ref, (zl, full, y, zh, k), near_y[d]) for d in (1, 3)]]
    t.received(*b1)
    b2 = push(gf_ref, (zl, full, y, zh, k), other_z)
    t.received(*a2b)
    a3.append(push(sf_ref, (1 - zl, full, y, zh, k), cross))
    a4a.append([push(sf_ref, (1 - zl, full, y, zh, k), near_y[d]) for d in (1, 3)])
    t.received(b2)
    b3 = {d: push(gf_ref, (full, full, y, zh, k), near_y[d]) for d in (1, 3, 2)}
    b4 = {0: push(gf_ref, (full, full, y, zh, k), cross)}
    home += [share(ref, other) for ref in (sf_ref, gf_ref)]
    home += [share(ref, (full, lax.rem(x + d, 4), y, zh, k)) for d in (1, 2, 3) for ref in (sf_ref, gf_ref)]
    batch()
    t.received(*home)
    group_sums()
    slice_rows = pl.ds(pl.multiple_of((me * 2 + k) * 32, 32), 32)
    y_parts = [t.start(part.at[slice_rows], from_y.at[d - 1], near_y[d]) for d in (1, 2, 3)]

    t.received(a3[0])
    a4b = [[push(sf_ref, (1 - zl, full, y, 1 - zh, k), near_y[d]) for d in (1, 3)]]
    t.received(a3[1])
    a4b.append([push(sf_ref, (zl, full, y, 1 - zh, k), near_y[d]) for d in (1, 3)])
    ready = {0: [share(sf_ref, (full, full, y, 1 - zh, k))]}
    batch()
    t.received(*y_parts)
    y_sum[...] = part[slice_rows, :] + from_y[0] + from_y[1] + from_y[2]
    z_part = t.start(y_sum, from_z, flip)

    source = {1: lax.rem(y + 3, 4), 3: lax.rem(y + 1, 4), 2: lax.rem(y + 2, 4)}
    far_own, far_other = [], []
    for half, a in ((0, zl), (1, 1 - zl)):
        t.received(a4a[half][0])
        far_own.append(push(sf_ref, (a, full, source[1], zh, k), near_y[1]))
    t.received(z_part)
    sums[zl, x, k] = y_sum[...] + from_z[...]
    x_sums = [push(sums, (zl, x, k), to) for to in near_x]
    for d in (1, 3):
        t.received(b3[d])
        b4[d] = push(gf_ref, (full, full, source[d], zh, k), cross)
        ready[d] = [b4[d], share(gf_ref, (full, full, source[d], zh, k))]
    t.received(a4a[0][1], a4a[1][1])
    for d in (1, 3):
        ready[d].append(share(sf_ref, (full, full, source[d], zh, k)))
    batch()
    t.received(*x_sums)
    z_sums = push(sums, (zl, full, k), other_z)
    t.received(b3[2])
    b4[2] = push(gf_ref, (full, full, source[2], zh, k), cross)
    ready[2] = [b4[2], share(gf_ref, (full, full, source[2], zh, k))]
    batch()
    t.received(z_sums)
    sib_sums = push(sums, (full, full, k), sib)
    t.received(b4[0])
    ready[0].append(share(gf_ref, (full, full, y, 1 - zh, k)))
    batch()
    t.received(sib_sums)
    invert_upper(sums[...].reshape(512, 768)[:, :512], inverse)
    for half, a in ((0, 1 - zl), (1, zl)):
        t.received(a4b[half][1])
        far_other.append(push(sf_ref, (a, full, source[3], 1 - zh, k), near_y[3]))
    t.received(a4b[0][0], a4b[1][0])
    for d in (1, 3):
        ready[d].append(share(sf_ref, (full, full, source[d], 1 - zh, k)))
    batch()
    mine.wait()
    for slots in batches[:4]:
        t.received(*slots)
    t.received(*ready[0])
    add_products(y, 0, 4 * piece)
    t.received(*far_own)
    ready[2].append(share(sf_ref, (full, full, source[2], zh, k)))
    for d in (1, 3):
        t.received(b4[d])
        ready[d].append(share(gf_ref, (full, full, source[d], 1 - zh, k)))
    for d in (1, 3):
        t.received(*ready[d])
        add_products(source[d], 0, 4 * piece)
    t.received(b4[2])
    ready[2].append(share(gf_ref, (full, full, source[2], 1 - zh, k)))
    t.received(*far_other)
    ready[2].append(share(sf_ref, (full, full, source[2], 1 - zh, k)))
    for slots in batches[4:]:
        t.received(*slots)
    for block in (y, source[1], source[3]):
        add_products(block, 4 * piece, rows)
    t.finish()
    add_products(source[2], 0, rows)
    coefficients = exact(total[:, :512], inverse[...]).astype(jnp.bfloat16)
    coef_ref[...] = coefficients
    changed = exact(coefficients.astype(jnp.float32), sums[...].reshape(512, 768)[:, 512:])
    rot_ref[...] = (total[:, 512:] - changed).astype(jnp.bfloat16)


def exchange(eigenvectors, sets, gradient):
    blocks = (2, 4, 4, 2, 2)
    rows, width = eigenvectors.shape[0] // 8, eigenvectors.shape[1]
    any_space = pl.BlockSpec(memory_space=pl.ANY)
    vmem = pl.BlockSpec(memory_space=pltpu.VMEM)
    return pl.pallas_call(
        exchange_kernel,
        out_shape=(
            jax.ShapeDtypeStruct((rows, 8 * width), jnp.bfloat16),
            jax.ShapeDtypeStruct(blocks + sets.shape, jnp.bfloat16),
            jax.ShapeDtypeStruct(blocks + gradient.shape, jnp.bfloat16),
            jax.ShapeDtypeStruct((rows, 512), jnp.bfloat16),
            jax.ShapeDtypeStruct((rows, 256), jnp.bfloat16),
        ),
        in_specs=[any_space] * 3,
        out_specs=(any_space,) * 3 + (vmem,) * 2,
        scratch_shapes=[
            pltpu.SemaphoreType.DMA((SLOTS,)),
            pltpu.SemaphoreType.DMA((SLOTS,)),
            pltpu.SemaphoreType.DMA((3,)),
            pltpu.VMEM((512, 768), jnp.float32),
            pltpu.VMEM((3, 32, 768), jnp.float32),
            pltpu.VMEM((32, 768), jnp.float32),
            pltpu.VMEM((32, 768), jnp.float32),
            pltpu.VMEM((2, 4, 2, 32, 768), jnp.float32),
            pltpu.VMEM((512, 512), jnp.float32),
            pltpu.VMEM((rows, 768), jnp.float32),
        ],
        compiler_params=pltpu.CompilerParams(
            collective_id=0, has_side_effects=True, vmem_limit_bytes=48 * 1024 * 1024
        ),
        name="exchange",
    )(eigenvectors, sets, gradient)


def update_kernel(coef_ref, x_ref, s_ref, g_ref, out_ref):
    across = (((1,), (1,)), ((), ()))
    update = lax.dot_general(
        coef_ref[:, :SPLIT], s_ref[...], across, preferred_element_type=jnp.float32
    ) + lax.dot_general(
        coef_ref[:, SPLIT:], g_ref[...], across, preferred_element_type=jnp.float32
    )
    out_ref[...] = (x_ref[...].astype(jnp.float32) - update).astype(jnp.bfloat16)


def renew(coefficients, slab, sets, gradient):
    rows, order = slab.shape
    block = order // 16
    return pl.pallas_call(
        update_kernel,
        grid=(16,),
        out_shape=jax.ShapeDtypeStruct(slab.shape, jnp.bfloat16),
        in_specs=[
            pl.BlockSpec(coefficients.shape, lambda i: (0, 0)),
            pl.BlockSpec((rows, block), lambda i: (0, i)),
            pl.BlockSpec((block, SPLIT), lambda i: (i, 0)),
            pl.BlockSpec((block, UPPER), lambda i: (i, 0)),
        ],
        out_specs=pl.BlockSpec((rows, block), lambda i: (0, i)),
        compiler_params=pltpu.CompilerParams(vmem_limit_bytes=32 * 1024 * 1024),
        name="renew",
    )(coefficients, slab, sets, gradient)


def body(eigenvectors, reflectors_first, reflectors_second, forget_gradient):
    sets = jnp.concatenate([reflectors_first, reflectors_second[:, :UPPER]], axis=1)
    rest = jnp.concatenate([reflectors_second[:, UPPER:], forget_gradient.T], axis=1)
    slab, all_sets, all_rest, coefficients, rotated = exchange(eigenvectors, sets, rest)
    renewed = renew(
        coefficients, slab, all_sets.reshape(-1, SPLIT), all_rest.reshape(-1, rest.shape[1])
    )
    return (renewed, rotated)


def solution(mesh):
    return jax.shard_map(
        body,
        mesh=mesh,
        in_specs=(
            P("col", "row"),
            P(("row", "col"), None),
            P(("row", "col"), None),
            P(None, ("row", "col")),
        ),
        out_specs=(P(("col", "row"), None), P(("col", "row"), None)),
        check_vma=False,
    )
```

```python
import jax
import jax.numpy as jnp
from jax import lax
from jax.experimental import pallas as pl
from jax.experimental.pallas import tpu as pltpu
from jax.sharding import PartitionSpec as P

MESH = pl.DeviceIdType.MESH
HIGH = lax.Precision.HIGHEST
BATCHES = 7
SLOTS = 160
SPLIT = 512


def exact(left_side, right_side):
    return jnp.dot(left_side, right_side, precision=HIGH, preferred_element_type=jnp.float32)


def inner_products(left_side, right_side):
    return lax.dot_general(
        left_side, right_side, (((0,), (0,)), ((), ())), preferred_element_type=jnp.float32
    )


def invert_upper(gram, inverse_ref):
    half = gram.shape[0] // 2
    rows = lax.broadcasted_iota(jnp.int32, (half, half), 0)
    cols = lax.broadcasted_iota(jnp.int32, (half, half), 1)
    parts = [gram[:half, :half], gram[half:, half:]]
    inverses = [jnp.where(rows == cols, 2.0 / part, 0.0) for part in parts]
    for level in range(half.bit_length() - 1):
        row_block, col_block = lax.shift_right_logical(rows, level), lax.shift_right_logical(cols, level)
        corner = (row_block + 1 == col_block) & ((row_block & 1) == 0)
        corners = [jnp.where(corner, part, 0.0) for part in parts]
        steps = [exact(c, i) for c, i in zip(corners, inverses)]
        inverses = [i - exact(i, s) for i, s in zip(inverses, steps)]
    cross = exact(inverses[0], exact(gram[:half, half:], inverses[1]))
    inverse_ref[:half, :half] = inverses[0]
    inverse_ref[half:, half:] = inverses[1]
    inverse_ref[:half, half:] = -cross
    inverse_ref[half:, :half] = jnp.zeros((half, half), jnp.float32)


def place():
    row, col = lax.axis_index("row"), lax.axis_index("col")
    return row // 4, row % 4, col // 4, (col // 2) % 2, col % 2


def device(zl, x, y, zh, k):
    return (zl * 4 + lax.rem(x + 4, 4), lax.rem(y + 4, 4) * 4 + zh * 2 + k)


class Transfers:
    def __init__(self, send_sem, recv_sem):
        self.send_sem, self.recv_sem = send_sem, recv_sem
        self.count = 0
        self.pending_send, self.pending_recv = {}, {}

    def start(self, source, target, to):
        slot = self.count
        self.count += 1
        copy = pltpu.make_async_remote_copy(
            source, target, self.send_sem.at[slot], self.recv_sem.at[slot],
            device_id=to, device_id_type=MESH,
        )
        copy.start()
        self.pending_send[slot] = copy
        self.pending_recv[slot] = copy
        return slot

    def received(self, *slots):
        for slot in slots:
            if slot in self.pending_recv:
                self.pending_recv.pop(slot).wait_recv()

    def finish(self):
        self.received(*list(self.pending_recv))
        for copy in self.pending_send.values():
            copy.wait_send()


def exchange_kernel(
    e_ref, s_ref, g_ref, x_ref, sf_ref, gf_ref, coef_ref, rot_ref,
    send_sem, recv_sem, local_sem, part, from_y, y_sum, from_z, sums, inverse, total,
):
    zl, x, y, zh, k = place()
    me = zl * 4 + x
    sib = device(zl, x, y, zh, 1 - k)
    cross = device(1 - zl, x, y, 1 - zh, k)
    flip = device(zl, x, y, 1 - zh, k)
    other_z = device(1 - zl, x, y, zh, k)
    near_x = [device(zl, x + d, y, zh, k) for d in (1, 3, 2)]
    near_y = {d: device(zl, x, y + d, zh, k) for d in (1, 3, 2)}
    partners = [device(a, x + d, y, zh, k) for a, d in
                [(1 - zl, 0), (zl, 1), (zl, 3), (1 - zl, 1), (1 - zl, 3), (zl, 2), (1 - zl, 2)]]
    barrier = pltpu.get_barrier_semaphore()
    everyone = partners + [sib, cross, flip] + list(near_y.values())
    for to in everyone:
        pl.semaphore_signal(barrier, inc=1, device_id=to, device_id_type=MESH)
    pl.semaphore_wait(barrier, len(everyone))

    t = Transfers(send_sem, recv_sem)
    rows, width = x_ref.shape[0], e_ref.shape[1]
    own_columns = pl.ds(pl.multiple_of(me * width, 128), width)
    piece = rows // BATCHES
    batches = []
    full = slice(None)

    def batch():
        q = len(batches)
        slots = []
        for to in partners:
            source = e_ref.at[pl.ds(pl.multiple_of(to[0] * rows + q * piece, 16), piece)]
            slots.append(t.start(source, x_ref.at[pl.ds(q * piece, piece), own_columns], to))
        batches.append(slots)

    def push(ref, index, to):
        view = ref.at[index]
        return t.start(view, view, to)

    def share(ref, index):
        return push(ref, index, sib)

    mine = pltpu.make_async_copy(
        e_ref.at[pl.ds(pl.multiple_of(me * rows, 16), rows)], x_ref.at[:, own_columns], local_sem.at[0])
    mine_s = pltpu.make_async_copy(s_ref, sf_ref.at[zl, x, y, zh, k], local_sem.at[1])
    mine_g = pltpu.make_async_copy(g_ref, gf_ref.at[zl, x, y, zh, k], local_sem.at[2])

    def group_sums():
        part[...] = jnp.zeros_like(part)

        def step(s_block, g_block):
            s_value = s_block[...].reshape(-1, SPLIT)
            g_value = g_block[...].reshape(-1, g_block.shape[-1])
            part[:, :SPLIT] += inner_products(s_value, s_value)
            part[:, SPLIT:] += inner_products(s_value, g_value)

        def spec(ref):
            return pl.BlockSpec(
                (None, None, None, None, 2) + ref.shape[5:], lambda i: (i // 4, i % 4, y, zh, 0, 0, 0)
            )

        pltpu.emit_pipeline(step, grid=(8,), in_specs=[spec(sf_ref), spec(gf_ref)])(sf_ref, gf_ref)

    def add_products(y_block):
        def step(x_block, s_block, g_block):
            x_value = x_block[...]
            s_value = s_block[...].reshape(-1, SPLIT)
            g_value = g_block[...].reshape(-1, g_block.shape[-1])
            total[:, :SPLIT] += jnp.dot(x_value, s_value, preferred_element_type=jnp.float32)
            total[:, SPLIT:] += jnp.dot(x_value, g_value, preferred_element_type=jnp.float32)

        def spec(ref):
            return pl.BlockSpec(
                (None, None, None, 2, 2) + ref.shape[5:], lambda i: (i // 4, i % 4, y_block, 0, 0, 0, 0)
            )

        x_spec = pl.BlockSpec((rows, width // 4), lambda i: (0, i * 4 + y_block))
        pltpu.emit_pipeline(step, grid=(8,), in_specs=[x_spec, spec(sf_ref), spec(gf_ref)])(
            x_ref, sf_ref, gf_ref)

    mine_s.start()
    mine_g.start()
    own, other = (zl, x, y, zh, k), (1 - zl, x, y, zh, k)
    b1 = [t.start(g_ref, gf_ref.at[own], to) for to in near_x]
    a1 = t.start(s_ref, sf_ref.at[own], other_z)
    a2 = [t.start(s_ref, sf_ref.at[own], to) for to in near_x]
    home = [t.start(s_ref, sf_ref.at[own], sib), t.start(g_ref, gf_ref.at[own], sib)]
    batch()
    mine.start()
    total[...] = jnp.zeros_like(total)
    mine_s.wait()
    mine_g.wait()
    t.received(*b1)
    b2 = push(gf_ref, (zl, full, y, zh, k), other_z)
    t.received(a1)
    a2_other = [push(sf_ref, other, to) for to in near_x]
    t.received(b2)
    b4 = {0: push(gf_ref, (full, full, y, zh, k), cross)}
    b3 = {d: push(gf_ref, (full, full, y, zh, k), near_y[d]) for d in (1, 3)}
    t.received(*a2)
    a3 = [push(sf_ref, (zl, full, y, zh, k), cross)]
    a4 = [[push(sf_ref, (zl, full, y, zh, k), near_y[d]) for d in (1, 3)]]
    t.received(*a2_other)
    a3.append(push(sf_ref, (1 - zl, full, y, zh, k), cross))
    a4.append([push(sf_ref, (1 - zl, full, y, zh, k), near_y[d]) for d in (1, 3)])
    home += [share(ref, other) for ref in (sf_ref, gf_ref)]
    home += [share(ref, (full, lax.rem(x + d, 4), y, zh, k)) for d in (1, 2, 3) for ref in (sf_ref, gf_ref)]
    batch()
    t.received(*home)
    group_sums()
    slice_rows = pl.ds(pl.multiple_of((me * 2 + k) * 32, 32), 32)
    y_parts = [t.start(part.at[slice_rows], from_y.at[d - 1], near_y[d]) for d in (1, 2, 3)]
    batch()
    t.received(*y_parts)
    y_sum[...] = part[slice_rows, :] + from_y[0] + from_y[1] + from_y[2]
    z_part = t.start(y_sum, from_z, flip)
    t.received(z_part)
    sums[zl, x, k] = y_sum[...] + from_z[...]
    x_sums = [push(sums, (zl, x, k), to) for to in near_x]
    t.received(*x_sums)
    z_sums = push(sums, (zl, full, k), other_z)
    for _ in range(BATCHES - len(batches)):
        batch()
    t.received(a3[0])
    a5 = [[push(sf_ref, (1 - zl, full, y, 1 - zh, k), near_y[d]) for d in (1, 3)]]
    t.received(a3[1])
    a5.append([push(sf_ref, (zl, full, y, 1 - zh, k), near_y[d]) for d in (1, 3)])
    ready = {0: [share(sf_ref, (full, full, y, 1 - zh, k))]}
    t.received(z_sums)
    sib_sums = push(sums, (full, full, k), sib)
    rest_far = []
    source = {1: lax.rem(y + 3, 4), 3: lax.rem(y + 1, 4), 2: lax.rem(y + 2, 4)}
    for d in (1, 3):
        t.received(b3[d])
        b4[d] = push(gf_ref, (full, full, source[d], zh, k), cross)
        ready[d] = [share(gf_ref, (full, full, source[d], zh, k))]
        rest_far.append(push(gf_ref, (d // 2, full, source[d], zh, k), near_y[d]))
    t.received(b4[0])
    ready[0].append(share(gf_ref, (full, full, y, 1 - zh, k)))
    far_own, far_other = [], []
    for half, a in ((0, zl), (1, 1 - zl)):
        t.received(a4[half][0])
        far_own.append(push(sf_ref, (a, full, source[1], zh, k), near_y[1]))
    t.received(*rest_far)
    b4[2] = push(gf_ref, (full, full, source[2], zh, k), cross)
    share(gf_ref, (full, full, source[2], zh, k))
    t.received(a4[0][1], a4[1][1])
    for d in (1, 3):
        ready[d].append(share(sf_ref, (full, full, source[d], zh, k)))
    for half, a in ((0, 1 - zl), (1, zl)):
        t.received(a5[half][1])
        far_other.append(push(sf_ref, (a, full, source[3], 1 - zh, k), near_y[3]))
    t.received(a5[0][0], a5[1][0])
    for d in (1, 3):
        ready[d].append(share(sf_ref, (full, full, source[d], 1 - zh, k)))
    t.received(sib_sums)
    invert_upper(sums[...].reshape(512, 768)[:, :512], inverse)
    for d in (1, 3):
        t.received(b4[d])
        ready[d].append(share(gf_ref, (full, full, source[d], 1 - zh, k)))
    t.received(*far_own)
    share(sf_ref, (full, full, source[2], zh, k))
    mine.wait()
    for slots in batches:
        t.received(*slots)
    t.received(*ready[0])
    add_products(y)
    t.received(*ready[1])
    add_products(source[1])
    t.received(b4[2])
    share(gf_ref, (full, full, source[2], 1 - zh, k))
    t.received(*far_other)
    share(sf_ref, (full, full, source[2], 1 - zh, k))
    t.received(*ready[3])
    add_products(source[3])
    t.finish()
    add_products(source[2])
    coefficients = exact(total[:, :512], inverse[...]).astype(jnp.bfloat16)
    coef_ref[...] = coefficients
    changed = exact(coefficients.astype(jnp.float32), sums[...].reshape(512, 768)[:, 512:])
    rot_ref[...] = (total[:, 512:] - changed).astype(jnp.bfloat16)


def exchange(eigenvectors, sets, gradient):
    blocks = (2, 4, 4, 2, 2)
    rows, width = eigenvectors.shape[0] // 8, eigenvectors.shape[1]
    any_space = pl.BlockSpec(memory_space=pl.ANY)
    vmem = pl.BlockSpec(memory_space=pltpu.VMEM)
    return pl.pallas_call(
        exchange_kernel,
        out_shape=(
            jax.ShapeDtypeStruct((rows, 8 * width), jnp.bfloat16),
            jax.ShapeDtypeStruct(blocks + sets.shape, jnp.bfloat16),
            jax.ShapeDtypeStruct(blocks + gradient.shape, jnp.bfloat16),
            jax.ShapeDtypeStruct((rows, 512), jnp.bfloat16),
            jax.ShapeDtypeStruct((rows, 256), jnp.bfloat16),
        ),
        in_specs=[any_space] * 3,
        out_specs=(any_space,) * 3 + (vmem,) * 2,
        scratch_shapes=[
            pltpu.SemaphoreType.DMA((SLOTS,)),
            pltpu.SemaphoreType.DMA((SLOTS,)),
            pltpu.SemaphoreType.DMA((3,)),
            pltpu.VMEM((512, 768), jnp.float32),
            pltpu.VMEM((3, 32, 768), jnp.float32),
            pltpu.VMEM((32, 768), jnp.float32),
            pltpu.VMEM((32, 768), jnp.float32),
            pltpu.VMEM((2, 4, 2, 32, 768), jnp.float32),
            pltpu.VMEM((512, 512), jnp.float32),
            pltpu.VMEM((rows, 768), jnp.float32),
        ],
        compiler_params=pltpu.CompilerParams(
            collective_id=0, has_side_effects=True, vmem_limit_bytes=48 * 1024 * 1024
        ),
        name="exchange",
    )(eigenvectors, sets, gradient)


def body(eigenvectors, reflectors_first, reflectors_second, forget_gradient):
    sets = jnp.concatenate([reflectors_first, reflectors_second], axis=1)
    slab, all_sets, _, coefficients, rotated = exchange(eigenvectors, sets, forget_gradient.T)
    update = lax.dot_general(
        coefficients, all_sets.reshape(-1, sets.shape[1]), (((1,), (1,)), ((), ())),
        preferred_element_type=jnp.float32,
    )
    return ((slab.astype(jnp.float32) - update).astype(jnp.bfloat16), rotated)


def solution(mesh):
    return jax.shard_map(
        body,
        mesh=mesh,
        in_specs=(
            P("col", "row"),
            P(("row", "col"), None),
            P(("row", "col"), None),
            P(None, ("row", "col")),
        ),
        out_specs=(P(("col", "row"), None), P(("col", "row"), None)),
        check_vma=False,
    )
```

```python
import jax
import jax.numpy as jnp
from jax import lax
from jax.experimental import pallas as pl
from jax.experimental.pallas import tpu as pltpu
from jax.sharding import PartitionSpec as P

MESH = pl.DeviceIdType.MESH
HIGH = lax.Precision.HIGHEST
BATCHES = 8
SLOTS = 160
SPLIT = 512


def exact(left_side, right_side):
    return jnp.dot(left_side, right_side, precision=HIGH, preferred_element_type=jnp.float32)


def inner_products(left_side, right_side):
    return lax.dot_general(
        left_side, right_side, (((0,), (0,)), ((), ())), preferred_element_type=jnp.float32
    )


def invert_upper(gram, inverse_ref):
    half = gram.shape[0] // 2
    rows = lax.broadcasted_iota(jnp.int32, (half, half), 0)
    cols = lax.broadcasted_iota(jnp.int32, (half, half), 1)
    parts = [gram[:half, :half], gram[half:, half:]]
    inverses = [jnp.where(rows == cols, 2.0 / part, 0.0) for part in parts]
    for level in range(half.bit_length() - 1):
        row_block, col_block = lax.shift_right_logical(rows, level), lax.shift_right_logical(cols, level)
        corner = (row_block + 1 == col_block) & ((row_block & 1) == 0)
        corners = [jnp.where(corner, part, 0.0) for part in parts]
        steps = [exact(c, i) for c, i in zip(corners, inverses)]
        inverses = [i - exact(i, s) for i, s in zip(inverses, steps)]
    cross = exact(inverses[0], exact(gram[:half, half:], inverses[1]))
    inverse_ref[:half, :half] = inverses[0]
    inverse_ref[half:, half:] = inverses[1]
    inverse_ref[:half, half:] = -cross
    inverse_ref[half:, :half] = jnp.zeros((half, half), jnp.float32)


def place():
    row, col = lax.axis_index("row"), lax.axis_index("col")
    return row // 4, row % 4, col // 4, (col // 2) % 2, col % 2


def device(zl, x, y, zh, k):
    return (zl * 4 + lax.rem(x + 4, 4), lax.rem(y + 4, 4) * 4 + zh * 2 + k)


class Transfers:
    def __init__(self, send_sem, recv_sem):
        self.send_sem, self.recv_sem = send_sem, recv_sem
        self.count = 0
        self.pending_send, self.pending_recv = {}, {}

    def start(self, source, target, to):
        slot = self.count
        self.count += 1
        copy = pltpu.make_async_remote_copy(
            source, target, self.send_sem.at[slot], self.recv_sem.at[slot],
            device_id=to, device_id_type=MESH,
        )
        copy.start()
        self.pending_send[slot] = copy
        self.pending_recv[slot] = copy
        return slot

    def received(self, *slots):
        for slot in slots:
            if slot in self.pending_recv:
                self.pending_recv.pop(slot).wait_recv()

    def finish(self):
        self.received(*list(self.pending_recv))
        for copy in self.pending_send.values():
            copy.wait_send()


def exchange_kernel(
    e_ref, s_ref, g_ref, x_ref, sf_ref, gf_ref, coef_ref, rot_ref,
    send_sem, recv_sem, local_sem, part, from_y, y_sum, from_z, sums, inverse, total,
):
    zl, x, y, zh, k = place()
    me = zl * 4 + x
    sib = device(zl, x, y, zh, 1 - k)
    cross = device(1 - zl, x, y, 1 - zh, k)
    flip = device(zl, x, y, 1 - zh, k)
    other_z = device(1 - zl, x, y, zh, k)
    near_x = [device(zl, x + d, y, zh, k) for d in (1, 3, 2)]
    near_y = {d: device(zl, x, y + d, zh, k) for d in (1, 3, 2)}
    partners = [device(a, x + d, y, zh, k) for a, d in
                [(1 - zl, 0), (zl, 1), (zl, 3), (1 - zl, 1), (1 - zl, 3), (zl, 2), (1 - zl, 2)]]
    barrier = pltpu.get_barrier_semaphore()
    everyone = partners + [sib, cross, flip] + list(near_y.values())
    for to in everyone:
        pl.semaphore_signal(barrier, inc=1, device_id=to, device_id_type=MESH)
    pl.semaphore_wait(barrier, len(everyone))

    t = Transfers(send_sem, recv_sem)
    rows, width = x_ref.shape[0], e_ref.shape[1]
    own_columns = pl.ds(pl.multiple_of(me * width, 128), width)
    source = {1: lax.rem(y + 3, 4), 3: lax.rem(y + 1, 4), 2: lax.rem(y + 2, 4)}
    y_order = [y, source[1], source[3], source[2]]
    batches = []
    full = slice(None)

    def batch():
        q = len(batches)
        half, block = rows // 2, width // 4
        low, offset = (q % 2) * half, y_order[q // 2] * block
        slots = []
        for to in partners:
            source_rows = pl.ds(pl.multiple_of(to[0] * rows + low, 16), half)
            source_columns = pl.ds(pl.multiple_of(offset, 128), block)
            target_columns = pl.ds(pl.multiple_of(me * width + offset, 128), block)
            slots.append(t.start(
                e_ref.at[source_rows, source_columns], x_ref.at[pl.ds(low, half), target_columns], to))
        batches.append(slots)

    def push(ref, index, to):
        view = ref.at[index]
        return t.start(view, view, to)

    def share(ref, index):
        return push(ref, index, sib)

    mine = pltpu.make_async_copy(
        e_ref.at[pl.ds(pl.multiple_of(me * rows, 16), rows)], x_ref.at[:, own_columns], local_sem.at[0])
    mine_s = pltpu.make_async_copy(s_ref, sf_ref.at[zl, x, y, zh, k], local_sem.at[1])
    mine_g = pltpu.make_async_copy(g_ref, gf_ref.at[zl, x, y, zh, k], local_sem.at[2])

    def group_sums():
        part[...] = jnp.zeros_like(part)

        def step(s_block, g_block):
            s_value = s_block[...].reshape(-1, SPLIT)
            g_value = g_block[...].reshape(-1, g_block.shape[-1])
            part[:, :SPLIT] += inner_products(s_value, s_value)
            part[:, SPLIT:] += inner_products(s_value, g_value)

        def spec(ref):
            return pl.BlockSpec(
                (None, None, None, None, 2) + ref.shape[5:], lambda i: (i // 4, i % 4, y, zh, 0, 0, 0)
            )

        pltpu.emit_pipeline(step, grid=(8,), in_specs=[spec(sf_ref), spec(gf_ref)])(sf_ref, gf_ref)

    def add_products(y_block):
        def step(x_block, s_block, g_block):
            x_value = x_block[...]
            s_value = s_block[...].reshape(-1, SPLIT)
            g_value = g_block[...].reshape(-1, g_block.shape[-1])
            total[:, :SPLIT] += jnp.dot(x_value, s_value, preferred_element_type=jnp.float32)
            total[:, SPLIT:] += jnp.dot(x_value, g_value, preferred_element_type=jnp.float32)

        def spec(ref):
            return pl.BlockSpec(
                (None, None, None, 2, 2) + ref.shape[5:], lambda i: (i // 4, i % 4, y_block, 0, 0, 0, 0)
            )

        x_spec = pl.BlockSpec((rows, width // 4), lambda i: (0, i * 4 + y_block))
        pltpu.emit_pipeline(step, grid=(8,), in_specs=[x_spec, spec(sf_ref), spec(gf_ref)])(
            x_ref, sf_ref, gf_ref)

    mine_s.start()
    mine_g.start()
    own, other = (zl, x, y, zh, k), (1 - zl, x, y, zh, k)
    b1 = [t.start(g_ref, gf_ref.at[own], to) for to in near_x]
    a1 = t.start(s_ref, sf_ref.at[own], other_z)
    a2 = [t.start(s_ref, sf_ref.at[own], to) for to in near_x]
    home = [t.start(s_ref, sf_ref.at[own], sib), t.start(g_ref, gf_ref.at[own], sib)]
    batch()
    mine.start()
    total[...] = jnp.zeros_like(total)
    mine_s.wait()
    mine_g.wait()
    t.received(*b1)
    b2 = push(gf_ref, (zl, full, y, zh, k), other_z)
    t.received(a1)
    a2_other = [push(sf_ref, other, to) for to in near_x]
    t.received(b2)
    b4 = {0: push(gf_ref, (full, full, y, zh, k), cross)}
    b3 = {d: push(gf_ref, (full, full, y, zh, k), near_y[d]) for d in (1, 3)}
    t.received(*a2)
    a3 = [push(sf_ref, (zl, full, y, zh, k), cross)]
    a4 = [[push(sf_ref, (zl, full, y, zh, k), near_y[d]) for d in (1, 3)]]
    t.received(*a2_other)
    a3.append(push(sf_ref, (1 - zl, full, y, zh, k), cross))
    a4.append([push(sf_ref, (1 - zl, full, y, zh, k), near_y[d]) for d in (1, 3)])
    home += [share(ref, other) for ref in (sf_ref, gf_ref)]
    home += [share(ref, (full, lax.rem(x + d, 4), y, zh, k)) for d in (1, 2, 3) for ref in (sf_ref, gf_ref)]
    batch()
    t.received(*home)
    group_sums()
    slice_rows = pl.ds(pl.multiple_of((me * 2 + k) * 32, 32), 32)
    y_parts = [t.start(part.at[slice_rows], from_y.at[d - 1], near_y[d]) for d in (1, 2, 3)]
    batch()
    t.received(*y_parts)
    y_sum[...] = part[slice_rows, :] + from_y[0] + from_y[1] + from_y[2]
    z_part = t.start(y_sum, from_z, flip)
    t.received(z_part)
    sums[zl, x, k] = y_sum[...] + from_z[...]
    x_sums = [push(sums, (zl, x, k), to) for to in near_x]
    t.received(*x_sums)
    z_sums = push(sums, (zl, full, k), other_z)
    for _ in range(BATCHES - len(batches)):
        batch()
    t.received(a3[0])
    a5 = [[push(sf_ref, (1 - zl, full, y, 1 - zh, k), near_y[d]) for d in (1, 3)]]
    t.received(a3[1])
    a5.append([push(sf_ref, (zl, full, y, 1 - zh, k), near_y[d]) for d in (1, 3)])
    ready = {0: [share(sf_ref, (full, full, y, 1 - zh, k))]}
    t.received(z_sums)
    sib_sums = push(sums, (full, full, k), sib)
    rest_far = []
    for d in (1, 3):
        t.received(b3[d])
        b4[d] = push(gf_ref, (full, full, source[d], zh, k), cross)
        ready[d] = [share(gf_ref, (full, full, source[d], zh, k))]
        rest_far.append(push(gf_ref, (d // 2, full, source[d], zh, k), near_y[d]))
    t.received(b4[0])
    ready[0].append(share(gf_ref, (full, full, y, 1 - zh, k)))
    far_own, far_other = [], []
    for half, a in ((0, zl), (1, 1 - zl)):
        t.received(a4[half][0])
        far_own.append(push(sf_ref, (a, full, source[1], zh, k), near_y[1]))
    t.received(*rest_far)
    b4[2] = push(gf_ref, (full, full, source[2], zh, k), cross)
    share(gf_ref, (full, full, source[2], zh, k))
    t.received(a4[0][1], a4[1][1])
    for d in (1, 3):
        ready[d].append(share(sf_ref, (full, full, source[d], zh, k)))
    for half, a in ((0, 1 - zl), (1, zl)):
        t.received(a5[half][1])
        far_other.append(push(sf_ref, (a, full, source[3], 1 - zh, k), near_y[3]))
    t.received(a5[0][0], a5[1][0])
    for d in (1, 3):
        ready[d].append(share(sf_ref, (full, full, source[d], 1 - zh, k)))
    t.received(sib_sums)
    invert_upper(sums[...].reshape(512, 768)[:, :512], inverse)
    for d in (1, 3):
        t.received(b4[d])
        ready[d].append(share(gf_ref, (full, full, source[d], 1 - zh, k)))
    mine.wait()
    t.received(*ready[0], *batches[0], *batches[1])
    add_products(y)
    t.received(*far_own)
    share(sf_ref, (full, full, source[2], zh, k))
    t.received(*ready[1], *batches[2], *batches[3])
    add_products(source[1])
    t.received(b4[2])
    share(gf_ref, (full, full, source[2], 1 - zh, k))
    t.received(*far_other)
    share(sf_ref, (full, full, source[2], 1 - zh, k))
    t.received(*ready[3], *batches[4], *batches[5])
    add_products(source[3])
    t.finish()
    add_products(source[2])
    coefficients = exact(total[:, :512], inverse[...]).astype(jnp.bfloat16)
    coef_ref[...] = coefficients
    changed = exact(coefficients.astype(jnp.float32), sums[...].reshape(512, 768)[:, 512:])
    rot_ref[...] = (total[:, 512:] - changed).astype(jnp.bfloat16)


def exchange(eigenvectors, sets, gradient):
    blocks = (2, 4, 4, 2, 2)
    rows, width = eigenvectors.shape[0] // 8, eigenvectors.shape[1]
    any_space = pl.BlockSpec(memory_space=pl.ANY)
    vmem = pl.BlockSpec(memory_space=pltpu.VMEM)
    return pl.pallas_call(
        exchange_kernel,
        out_shape=(
            jax.ShapeDtypeStruct((rows, 8 * width), jnp.bfloat16),
            jax.ShapeDtypeStruct(blocks + sets.shape, jnp.bfloat16),
            jax.ShapeDtypeStruct(blocks + gradient.shape, jnp.bfloat16),
            jax.ShapeDtypeStruct((rows, 512), jnp.bfloat16),
            jax.ShapeDtypeStruct((rows, 256), jnp.bfloat16),
        ),
        in_specs=[any_space] * 3,
        out_specs=(any_space,) * 3 + (vmem,) * 2,
        scratch_shapes=[
            pltpu.SemaphoreType.DMA((SLOTS,)),
            pltpu.SemaphoreType.DMA((SLOTS,)),
            pltpu.SemaphoreType.DMA((3,)),
            pltpu.VMEM((512, 768), jnp.float32),
            pltpu.VMEM((3, 32, 768), jnp.float32),
            pltpu.VMEM((32, 768), jnp.float32),
            pltpu.VMEM((32, 768), jnp.float32),
            pltpu.VMEM((2, 4, 2, 32, 768), jnp.float32),
            pltpu.VMEM((512, 512), jnp.float32),
            pltpu.VMEM((rows, 768), jnp.float32),
        ],
        compiler_params=pltpu.CompilerParams(
            collective_id=0, has_side_effects=True, vmem_limit_bytes=48 * 1024 * 1024
        ),
        name="exchange",
    )(eigenvectors, sets, gradient)


def body(eigenvectors, reflectors_first, reflectors_second, forget_gradient):
    sets = jnp.concatenate([reflectors_first, reflectors_second], axis=1)
    slab, all_sets, _, coefficients, rotated = exchange(eigenvectors, sets, forget_gradient.T)
    update = lax.dot_general(
        coefficients, all_sets.reshape(-1, sets.shape[1]), (((1,), (1,)), ((), ())),
        preferred_element_type=jnp.float32,
    )
    return ((slab.astype(jnp.float32) - update).astype(jnp.bfloat16), rotated)


def solution(mesh):
    return jax.shard_map(
        body,
        mesh=mesh,
        in_specs=(
            P("col", "row"),
            P(("row", "col"), None),
            P(("row", "col"), None),
            P(None, ("row", "col")),
        ),
        out_specs=(P(("col", "row"), None), P(("col", "row"), None)),
        check_vma=False,
    )
```

```python
import jax
import jax.numpy as jnp
from jax import lax
from jax.experimental import pallas as pl
from jax.experimental.pallas import tpu as pltpu
from jax.sharding import PartitionSpec as P

MESH = pl.DeviceIdType.MESH
HIGH = lax.Precision.HIGHEST
BATCHES = 8
SLOTS = 160
SPLIT = 512


def exact(left_side, right_side):
    return jnp.dot(left_side, right_side, precision=HIGH, preferred_element_type=jnp.float32)


def inner_products(left_side, right_side):
    return lax.dot_general(
        left_side, right_side, (((0,), (0,)), ((), ())), preferred_element_type=jnp.float32
    )


def invert_upper(gram, inverse_ref):
    half = gram.shape[0] // 2
    rows = lax.broadcasted_iota(jnp.int32, (half, half), 0)
    cols = lax.broadcasted_iota(jnp.int32, (half, half), 1)
    parts = [gram[:half, :half], gram[half:, half:]]
    inverses = [jnp.where(rows == cols, 2.0 / part, 0.0) for part in parts]
    for level in range(half.bit_length() - 1):
        row_block, col_block = lax.shift_right_logical(rows, level), lax.shift_right_logical(cols, level)
        corner = (row_block + 1 == col_block) & ((row_block & 1) == 0)
        corners = [jnp.where(corner, part, 0.0) for part in parts]
        steps = [exact(c, i) for c, i in zip(corners, inverses)]
        inverses = [i - exact(i, s) for i, s in zip(inverses, steps)]
    cross = exact(inverses[0], exact(gram[:half, half:], inverses[1]))
    inverse_ref[:half, :half] = inverses[0]
    inverse_ref[half:, half:] = inverses[1]
    inverse_ref[:half, half:] = -cross
    inverse_ref[half:, :half] = jnp.zeros((half, half), jnp.float32)


def place():
    row, col = lax.axis_index("row"), lax.axis_index("col")
    return row // 4, row % 4, col // 4, (col // 2) % 2, col % 2


def device(zl, x, y, zh, k):
    return (zl * 4 + lax.rem(x + 4, 4), lax.rem(y + 4, 4) * 4 + zh * 2 + k)


class Transfers:
    def __init__(self, send_sem, recv_sem):
        self.send_sem, self.recv_sem = send_sem, recv_sem
        self.count = 0
        self.pending_send, self.pending_recv = {}, {}

    def start(self, source, target, to):
        slot = self.count
        self.count += 1
        copy = pltpu.make_async_remote_copy(
            source, target, self.send_sem.at[slot], self.recv_sem.at[slot],
            device_id=to, device_id_type=MESH,
        )
        copy.start()
        self.pending_send[slot] = copy
        self.pending_recv[slot] = copy
        return slot

    def received(self, *slots):
        for slot in slots:
            if slot in self.pending_recv:
                self.pending_recv.pop(slot).wait_recv()

    def finish(self):
        self.received(*list(self.pending_recv))
        for copy in self.pending_send.values():
            copy.wait_send()


def exchange_kernel(
    e_ref, s1_ref, s2_ref, g_ref, x_ref, sf_ref, gf_ref, coef_ref, rot_ref,
    send_sem, recv_sem, local_sem, part, from_y, y_sum, from_z, sums, inverse, total,
):
    zl, x, y, zh, k = place()
    me = zl * 4 + x
    sib = device(zl, x, y, zh, 1 - k)
    cross = device(1 - zl, x, y, 1 - zh, k)
    flip = device(zl, x, y, 1 - zh, k)
    other_z = device(1 - zl, x, y, zh, k)
    near_x = [device(zl, x + d, y, zh, k) for d in (1, 3, 2)]
    near_y = {d: device(zl, x, y + d, zh, k) for d in (1, 3, 2)}
    partners = [device(a, x + d, y, zh, k) for a, d in
                [(1 - zl, 0), (zl, 1), (zl, 3), (1 - zl, 1), (1 - zl, 3), (zl, 2), (1 - zl, 2)]]
    barrier = pltpu.get_barrier_semaphore()
    everyone = partners + [sib, cross, flip] + list(near_y.values())
    for to in everyone:
        pl.semaphore_signal(barrier, inc=1, device_id=to, device_id_type=MESH)
    pl.semaphore_wait(barrier, len(everyone))

    t = Transfers(send_sem, recv_sem)
    rows, width = x_ref.shape[0], e_ref.shape[1]
    own_columns = pl.ds(pl.multiple_of(me * width, 128), width)
    source = {1: lax.rem(y + 3, 4), 3: lax.rem(y + 1, 4), 2: lax.rem(y + 2, 4)}
    y_order = [y, source[1], source[3], source[2]]
    batches = []
    full = slice(None)

    def batch():
        q = len(batches)
        half, block = rows // 2, width // 4
        low, offset = (q % 2) * half, y_order[q // 2] * block
        slots = []
        for to in partners:
            source_rows = pl.ds(pl.multiple_of(to[0] * rows + low, 16), half)
            source_columns = pl.ds(pl.multiple_of(offset, 128), block)
            target_columns = pl.ds(pl.multiple_of(me * width + offset, 128), block)
            slots.append(t.start(
                e_ref.at[source_rows, source_columns], x_ref.at[pl.ds(low, half), target_columns], to))
        batches.append(slots)

    def push(ref, index, to):
        view = ref.at[index]
        return t.start(view, view, to)

    def share(ref, index):
        return push(ref, index, sib)

    mine = pltpu.make_async_copy(
        e_ref.at[pl.ds(pl.multiple_of(me * rows, 16), rows)], x_ref.at[:, own_columns], local_sem.at[0])
    mine_s = [
        pltpu.make_async_copy(
            ref, sf_ref.at[zl, x, y, zh, k, :, pl.ds(i * ref.shape[1], ref.shape[1])], local_sem.at[1 + i])
        for i, ref in enumerate((s1_ref, s2_ref))]
    mine_g = pltpu.make_async_copy(g_ref, gf_ref.at[zl, x, y, zh, k], local_sem.at[3])

    def group_sums():
        part[...] = jnp.zeros_like(part)

        def step(s_block, g_block):
            s_value = s_block[...].reshape(-1, SPLIT)
            g_value = g_block[...].reshape(-1, g_block.shape[-1])
            part[:, :SPLIT] += inner_products(s_value, s_value)
            part[:, SPLIT:] += inner_products(s_value, g_value)

        def spec(ref):
            return pl.BlockSpec(
                (None, None, None, None, 2) + ref.shape[5:], lambda i: (i // 4, i % 4, y, zh, 0, 0, 0)
            )

        pltpu.emit_pipeline(step, grid=(8,), in_specs=[spec(sf_ref), spec(gf_ref)])(sf_ref, gf_ref)

    def add_products(y_block):
        def step(x_block, s_block, g_block):
            x_value = x_block[...]
            s_value = s_block[...].reshape(-1, SPLIT)
            g_value = g_block[...].reshape(-1, g_block.shape[-1])
            total[:, :SPLIT] += jnp.dot(x_value, s_value, preferred_element_type=jnp.float32)
            total[:, SPLIT:] += jnp.dot(x_value, g_value, preferred_element_type=jnp.float32)

        def spec(ref):
            return pl.BlockSpec(
                (None, None, None, 2, 2) + ref.shape[5:], lambda i: (i // 4, i % 4, y_block, 0, 0, 0, 0)
            )

        x_spec = pl.BlockSpec((rows, width // 4), lambda i: (0, i * 4 + y_block))
        pltpu.emit_pipeline(step, grid=(8,), in_specs=[x_spec, spec(sf_ref), spec(gf_ref)])(
            x_ref, sf_ref, gf_ref)

    for copy in mine_s:
        copy.start()
    mine_g.start()
    own, other = (zl, x, y, zh, k), (1 - zl, x, y, zh, k)
    b1 = [t.start(g_ref, gf_ref.at[own], to) for to in near_x]
    for copy in mine_s:
        copy.wait()
    a1 = push(sf_ref, own, other_z)
    a2 = [push(sf_ref, own, to) for to in near_x]
    home = [push(sf_ref, own, sib), t.start(g_ref, gf_ref.at[own], sib)]
    mine.start()
    total[...] = jnp.zeros_like(total)
    mine_g.wait()
    t.received(*b1)
    b2 = push(gf_ref, (zl, full, y, zh, k), other_z)
    t.received(a1)
    a2_other = [push(sf_ref, other, to) for to in near_x]
    batch()
    t.received(b2)
    b4 = {0: push(gf_ref, (full, full, y, zh, k), cross)}
    b3 = {d: push(gf_ref, (full, full, y, zh, k), near_y[d]) for d in (1, 3)}
    t.received(*a2)
    a3 = [push(sf_ref, (zl, full, y, zh, k), cross)]
    a4 = [[push(sf_ref, (zl, full, y, zh, k), near_y[d]) for d in (1, 3)]]
    t.received(*a2_other)
    a3.append(push(sf_ref, (1 - zl, full, y, zh, k), cross))
    a4.append([push(sf_ref, (1 - zl, full, y, zh, k), near_y[d]) for d in (1, 3)])
    home += [share(ref, other) for ref in (sf_ref, gf_ref)]
    home += [share(ref, (full, lax.rem(x + d, 4), y, zh, k)) for d in (1, 2, 3) for ref in (sf_ref, gf_ref)]
    batch()
    t.received(*home)
    group_sums()
    slice_rows = pl.ds(pl.multiple_of((me * 2 + k) * 32, 32), 32)
    y_parts = [t.start(part.at[slice_rows], from_y.at[d - 1], near_y[d]) for d in (1, 2, 3)]
    batch()
    t.received(*y_parts)
    y_sum[...] = part[slice_rows, :] + from_y[0] + from_y[1] + from_y[2]
    z_part = t.start(y_sum, from_z, flip)
    t.received(z_part)
    sums[zl, x, k] = y_sum[...] + from_z[...]
    x_sums = [push(sums, (zl, x, k), to) for to in near_x]
    t.received(*x_sums)
    z_sums = push(sums, (zl, full, k), other_z)
    for _ in range(BATCHES - len(batches)):
        batch()
    t.received(a3[0])
    a5 = [[push(sf_ref, (1 - zl, full, y, 1 - zh, k), near_y[d]) for d in (1, 3)]]
    t.received(a3[1])
    a5.append([push(sf_ref, (zl, full, y, 1 - zh, k), near_y[d]) for d in (1, 3)])
    ready = {0: [share(sf_ref, (full, full, y, 1 - zh, k))]}
    t.received(z_sums)
    sib_sums = push(sums, (full, full, k), sib)
    rest_far = []
    for d in (1, 3):
        t.received(b3[d])
        b4[d] = push(gf_ref, (full, full, source[d], zh, k), cross)
        ready[d] = [share(gf_ref, (full, full, source[d], zh, k))]
        rest_far.append(push(gf_ref, (d // 2, full, source[d], zh, k), near_y[d]))
    t.received(b4[0])
    ready[0].append(share(gf_ref, (full, full, y, 1 - zh, k)))
    far_own, far_other = [], []
    for half, a in ((0, zl), (1, 1 - zl)):
        t.received(a4[half][0])
        far_own.append(push(sf_ref, (a, full, source[1], zh, k), near_y[1]))
    t.received(*rest_far)
    b4[2] = push(gf_ref, (full, full, source[2], zh, k), cross)
    share(gf_ref, (full, full, source[2], zh, k))
    t.received(a4[0][1], a4[1][1])
    for d in (1, 3):
        ready[d].append(share(sf_ref, (full, full, source[d], zh, k)))
    for half, a in ((0, 1 - zl), (1, zl)):
        t.received(a5[half][1])
        far_other.append(push(sf_ref, (a, full, source[3], 1 - zh, k), near_y[3]))
    t.received(a5[0][0], a5[1][0])
    for d in (1, 3):
        ready[d].append(share(sf_ref, (full, full, source[d], 1 - zh, k)))
    t.received(sib_sums)
    invert_upper(sums[...].reshape(512, 768)[:, :512], inverse)
    for d in (1, 3):
        t.received(b4[d])
        ready[d].append(share(gf_ref, (full, full, source[d], 1 - zh, k)))
    mine.wait()
    t.received(*ready[0], *batches[0], *batches[1])
    add_products(y)
    t.received(*far_own)
    share(sf_ref, (full, full, source[2], zh, k))
    t.received(*ready[1], *batches[2], *batches[3])
    add_products(source[1])
    t.received(b4[2])
    share(gf_ref, (full, full, source[2], 1 - zh, k))
    t.received(*far_other)
    share(sf_ref, (full, full, source[2], 1 - zh, k))
    t.received(*ready[3], *batches[4], *batches[5])
    add_products(source[3])
    t.finish()
    add_products(source[2])
    coefficients = exact(total[:, :512], inverse[...]).astype(jnp.bfloat16)
    coef_ref[...] = coefficients
    changed = exact(coefficients.astype(jnp.float32), sums[...].reshape(512, 768)[:, 512:])
    rot_ref[...] = (total[:, 512:] - changed).astype(jnp.bfloat16)


def exchange(eigenvectors, first, second, gradient):
    blocks = (2, 4, 4, 2, 2)
    rows, width = eigenvectors.shape[0] // 8, eigenvectors.shape[1]
    any_space = pl.BlockSpec(memory_space=pl.ANY)
    vmem = pl.BlockSpec(memory_space=pltpu.VMEM)
    return pl.pallas_call(
        exchange_kernel,
        out_shape=(
            jax.ShapeDtypeStruct((rows, 8 * width), jnp.bfloat16),
            jax.ShapeDtypeStruct(blocks + (first.shape[0], SPLIT), jnp.bfloat16),
            jax.ShapeDtypeStruct(blocks + gradient.shape, jnp.bfloat16),
            jax.ShapeDtypeStruct((rows, 512), jnp.bfloat16),
            jax.ShapeDtypeStruct((rows, 256), jnp.bfloat16),
        ),
        in_specs=[any_space] * 4,
        out_specs=(any_space,) * 3 + (vmem,) * 2,
        scratch_shapes=[
            pltpu.SemaphoreType.DMA((SLOTS,)),
            pltpu.SemaphoreType.DMA((SLOTS,)),
            pltpu.SemaphoreType.DMA((4,)),
            pltpu.VMEM((512, 768), jnp.float32),
            pltpu.VMEM((3, 32, 768), jnp.float32),
            pltpu.VMEM((32, 768), jnp.float32),
            pltpu.VMEM((32, 768), jnp.float32),
            pltpu.VMEM((2, 4, 2, 32, 768), jnp.float32),
            pltpu.VMEM((512, 512), jnp.float32),
            pltpu.VMEM((rows, 768), jnp.float32),
        ],
        compiler_params=pltpu.CompilerParams(
            collective_id=0, has_side_effects=True, vmem_limit_bytes=48 * 1024 * 1024
        ),
        name="exchange",
    )(eigenvectors, first, second, gradient)


def body(eigenvectors, reflectors_first, reflectors_second, forget_gradient):
    slab, all_sets, _, coefficients, rotated = exchange(
        eigenvectors, reflectors_first, reflectors_second, forget_gradient.T
    )
    update = lax.dot_general(
        coefficients, all_sets.reshape(-1, SPLIT), (((1,), (1,)), ((), ())),
        preferred_element_type=jnp.float32,
    )
    return ((slab.astype(jnp.float32) - update).astype(jnp.bfloat16), rotated)


def solution(mesh):
    return jax.shard_map(
        body,
        mesh=mesh,
        in_specs=(
            P("col", "row"),
            P(("row", "col"), None),
            P(("row", "col"), None),
            P(None, ("row", "col")),
        ),
        out_specs=(P(("col", "row"), None), P(("col", "row"), None)),
        check_vma=False,
    )
```
